32 devices in a mesh: seq: 8 (over y, x, core), tp: 4 (over z).
Axes of the slice: x: 2, y: 2, z: 4, core: 2. Of those that a mesh axis runs over, the one named last changes fastest.
Arguments:
- semantic_states: bfloat16 [2048, 3584], P('seq', 'tp'), may hold values from -6 to 6
- token_projection: bfloat16 [3584, 1024], P('tp'), may hold values from -0.09375 to 0.09375
- phase_offsets: float32 [4, 1024], replicated, may hold values from -6 to 6
- target_spectrum: float32 [8192, 80], P(('seq', 'tp')), may hold values from -6 to 6
- noise: float32 [8192, 80], P(('seq', 'tp')), may hold values from -6 to 6
- timestep: float32 [1], replicated, may hold values from 0.05 to 0.95
- frame_lift: bfloat16 [80, 1024], replicated, may hold values from -0.625 to 0.625
- time_weight: float32 [256, 2048], replicated, may hold values from -0.375 to 0.375
- attention_weight: bfloat16 [1024, 3, 1024], P(None, None, 'tp'), may hold values from -2 to 2
- head_mixing: bfloat16 [1024, 1024], P('tp'), may hold values from -0.1875 to 0.1875
- velocity_head: bfloat16 [1024, 80], replicated, may hold values from -0.1875 to 0.1875
- group_index: int32 [8192], replicated, may hold values from 0 to 127, never falling along the last dimension, each value on 1 to 128 neighbouring positions
- block_order: int32 [16], replicated, may hold values from 0 to 15, each once
Outputs:
- velocity: float32 [8192, 80], P(('seq', 'tp'))
The draws below stay inside these ranges and needn't reach their ends.
Inputs may be any that keep to these rules, and one draw needn't show every extreme that they name: `group_index`: Non-decreasing along the natural frame position; every group 0 to 127 holds 1 to 128 consecutive frames, one exactly 128. A permutation: stored block b holds the frames of natural block block_order[b] and the tokens of those frames.
All inputs are finite; a program needn't handle non-finite values.
Results may differ from the reference program's by a relative error of at most 0.006.
Values may be sent and summed in bfloat16 or wider, within the bound.
A program may use at most 64 MiB of HBM per device.

```python
import math
import jax
import jax.numpy as jnp
import numpy as np
from jax import lax

LLM_WIDTH = 3584
WIDTH = 1024
HEADS = 16
MEL_BINS = 80
TIME_FEATURES = 256
UPSAMPLE = 4
GROUP_MOST = 128
HEAD_DIM = 64
TOKENS = 2048
FRAMES = 8192
BLOCK = 512
BLOCKS = 16
GROUPS = 128


def draw_attention_weight(key, part):
    first = jax.random.fold_in(key, 0)
    base = jax.random.normal(first, (WIDTH, 3, WIDTH), jnp.float32) / math.sqrt(WIDTH)
    stacked = base
    return jnp.clip(stacked, -2.0, 2.0).astype(jnp.bfloat16)


def raised(array, stream_key, source, target, parts, factor):
    owner, partner = [(jnp.arange(array.shape[axis_at]) // (array.shape[axis_at] // parts)).reshape([-1 if axis == axis_at else 1 for axis in range(array.ndim)]) for axis_at in (source, target)]
    chosen = jax.random.permutation(stream_key, parts)[partner]
    strong = (owner == chosen) | (owner == (partner + parts // 2) % parts)
    return jnp.where(strong, factor * array, array)


def level_of(key, dims, cuts, smallest, high):
    factor_of, own = 1.0, jax.random.fold_in(key, 6)
    for position, shards_of in cuts:
        heights = jnp.exp(jax.random.uniform(jax.random.fold_in(own, position), (shards_of,), jnp.float32, smallest / len(cuts), high / len(cuts)))
        factor_of = factor_of * jnp.repeat(heights, dims[position] // shards_of).reshape([-1 if axis == position else 1 for axis in range(len(dims))])
    return factor_of


def profile(number_of, total, bound, slope):
    weights = [(1 << 20) // math.isqrt(grade ** slope) + 1 for grade in range(2, number_of + 1)]
    surplus, given = total - bound - (number_of - 1), [1] * (number_of - 1)
    while surplus > 0:
        free = [i for i in range(number_of - 1) if given[i] < bound]
        mass, budget = sum([weights[i] for i in free]), surplus
        for i in free:
            addition = min(bound - given[i], max(1, budget * weights[i] // mass), surplus)
            given[i] = given[i] + addition
            surplus = surplus - addition
    return np.array([bound] + given)


def uneven_parts(own_key, amount, total, bound, slope):
    if amount == 2:
        one = jax.random.randint(own_key, (), max(1, total - bound), min(bound, total - 1) + 1)
        return jnp.stack([one, total - one])
    tallies = jnp.asarray(profile(amount, total, bound, slope), jnp.int32)
    twos = (amount - 1) // 2
    donor, sink = tallies[1:1 + 2 * twos:2], tallies[2:2 + 2 * twos:2]
    slack = jnp.minimum(donor - 1, bound - sink)
    shifted = jax.random.randint(jax.random.fold_in(own_key, 1), (twos,), 0, 1 << 20) % (slack + 1)
    tallies = tallies.at[1:1 + 2 * twos:2].set(donor - shifted).at[2:2 + 2 * twos:2].set(sink + shifted)
    return tallies[jax.random.permutation(jax.random.fold_in(own_key, 2), amount)]


def normal_values(stream_key, dims, scale, most, cuts=(), held_as=jnp.bfloat16):
    result = scale * jax.random.normal(stream_key, dims, jnp.float32)
    if cuts:
        result = result * level_of(stream_key, dims, cuts, -0.22, 0.18)
    return jnp.clip(result, -most, most).astype(held_as)


def gaussian_with(stream_key, dims, width, most, shards, heavy, kind=jnp.bfloat16):
    array = width * jax.random.normal(stream_key, dims, jnp.float32)
    if shards:
        array = array * level_of(stream_key, dims, shards, -0.22, 0.18)
    return jnp.clip(raised(array, jax.random.fold_in(stream_key, 3), *heavy), -most, most).astype(kind)


def setup_inputs(seed: int = 0) -> dict:
    key_of = jax.random.split(jax.random.key(seed), 14)
    semantic_states = gaussian_with(key_of[0], (TOKENS, LLM_WIDTH), 1.0, 6.0, ((0, 8), (1, 4)), (1, 0, 8, 2.0))
    token_projection = normal_values(key_of[1], (LLM_WIDTH, WIDTH), LLM_WIDTH ** -0.5, 0.09375, ((0, 4),))
    phase_offsets = normal_values(key_of[2], (UPSAMPLE, WIDTH), 1.0, 6.0, (), jnp.float32)
    target_spectrum = normal_values(key_of[3], (FRAMES, MEL_BINS), 1.0, 6.0, ((0, 32),), jnp.float32)
    noise = normal_values(key_of[4], (FRAMES, MEL_BINS), 1.0, 6.0, ((0, 32),), jnp.float32)
    timestep = jnp.clip(jax.random.uniform(key_of[5], (1,), jnp.float32, 0.05, 0.95), 0.05, 0.95)
    frame_lift = normal_values(key_of[6], (MEL_BINS, WIDTH), MEL_BINS ** -0.5, 0.625)
    time_weight = normal_values(key_of[7], (TIME_FEATURES, 2 * WIDTH), TIME_FEATURES ** -0.5, 0.375, (), jnp.float32)
    attention_weight = draw_attention_weight(jax.random.fold_in(key_of[13], 71), 0)
    head_mixing = normal_values(key_of[9], (WIDTH, WIDTH), WIDTH ** -0.5, 0.1875, ((0, 4),))
    velocity_head = normal_values(key_of[10], (WIDTH, MEL_BINS), WIDTH ** -0.5, 0.1875)
    group_index = jnp.searchsorted(jnp.cumsum(uneven_parts(key_of[11], GROUPS, FRAMES, GROUP_MOST, 1)), jnp.arange(FRAMES), side="right").astype(jnp.int32)
    block_order = jax.random.permutation(key_of[12], BLOCKS).astype(jnp.int32)
    return {"semantic_states": semantic_states, "token_projection": token_projection, "phase_offsets": phase_offsets, "target_spectrum": target_spectrum, "noise": noise, "timestep": timestep, "frame_lift": frame_lift, "time_weight": time_weight, "attention_weight": attention_weight, "head_mixing": head_mixing, "velocity_head": velocity_head, "group_index": group_index, "block_order": block_order}


def layer_norm(values):
    center = values - lax.optimization_barrier(jnp.mean(values, axis=-1, keepdims=True))
    spread = lax.optimization_barrier(jnp.mean(center * center, axis=-1, keepdims=True))
    return center * lax.rsqrt(spread + 1e-06)

def time_modulation(timestep, time_weight):
    half_count = time_weight.shape[0] // 2
    rates = jnp.exp(-math.log(10000.0) * jnp.arange(half_count, dtype=jnp.float32) / half_count)
    angles = 1000.0 * timestep[0] * rates
    features = jnp.concatenate([jnp.cos(angles), jnp.sin(angles)])
    return jnp.dot(jax.nn.silu(features)[None, :], time_weight, precision=lax.Precision.HIGHEST)[0]

def reference(semantic_states, token_projection, phase_offsets, target_spectrum, noise, timestep, frame_lift, time_weight, attention_weight, head_mixing, velocity_head, group_index, block_order):
    cond = jnp.dot(semantic_states, token_projection, preferred_element_type=jnp.float32)
    moment = timestep[0]
    mixed = ((1.0 - moment) * noise + moment * target_spectrum).astype(jnp.bfloat16)
    lifted = jnp.dot(mixed, frame_lift, preferred_element_type=jnp.float32)
    start_state = (lifted.reshape(TOKENS, UPSAMPLE, WIDTH) + cond[:, None, :] + phase_offsets[None]).reshape(FRAMES, WIDTH)
    modulation = time_modulation(timestep, time_weight)
    normed = (layer_norm(start_state) * (1.0 + modulation[WIDTH:]) + modulation[:WIDTH]).astype(jnp.bfloat16)
    projected = jnp.dot(normed, attention_weight.reshape(WIDTH, 3 * WIDTH), preferred_element_type=jnp.float32).astype(jnp.bfloat16)
    projected = projected.reshape(FRAMES, 3, HEADS, HEAD_DIM)
    natural = (block_order[:, None].astype(jnp.int32) * BLOCK + jnp.arange(BLOCK, dtype=jnp.int32)[None, :]).reshape(FRAMES).astype(jnp.int32)
    frame_group = jnp.take(group_index, natural)
    factor = 1.0 / math.sqrt(HEAD_DIM)
    zero_index = jnp.zeros((), jnp.int32)

    def attend(index):
        block_id = (index // HEADS).astype(jnp.int32)
        head_id = (index % HEADS).astype(jnp.int32)
        row_start = (block_id * BLOCK).astype(jnp.int32)
        queries = lax.dynamic_slice(projected, (row_start, zero_index, head_id, zero_index), (BLOCK, 1, 1, HEAD_DIM))[:, 0, 0]
        keys = lax.dynamic_index_in_dim(projected[:, 1], head_id, 1, keepdims=False)
        values = lax.dynamic_index_in_dim(projected[:, 2], head_id, 1, keepdims=False)
        query_group = lax.dynamic_slice_in_dim(frame_group, row_start, BLOCK)
        scores = jnp.dot(queries, keys.T, preferred_element_type=jnp.float32) * factor
        allowed = frame_group[None, :] <= query_group[:, None]
        highest = lax.optimization_barrier(jnp.max(jnp.where(allowed, scores, -1e+30), axis=1))
        expo = jnp.where(allowed, jnp.exp(scores - highest[:, None]), 0.0)
        denominator = lax.optimization_barrier(jnp.sum(expo, axis=1))
        weights = expo.astype(jnp.bfloat16)
        return jnp.dot(weights, values, preferred_element_type=jnp.float32) / denominator[:, None]
    pieces = lax.map(attend, jnp.arange(BLOCKS * HEADS, dtype=jnp.int32))
    attended = pieces.reshape(BLOCKS, HEADS, BLOCK, HEAD_DIM).transpose(0, 2, 1, 3).reshape(FRAMES, WIDTH).astype(jnp.bfloat16)
    final_state = start_state + jnp.dot(attended, head_mixing, preferred_element_type=jnp.float32)
    closing = layer_norm(final_state).astype(jnp.bfloat16)
    return jnp.dot(closing, velocity_head, preferred_element_type=jnp.float32)
```

```python
import functools
import math

import jax
import jax.numpy as jnp
from jax import lax
from jax.experimental import pallas as pl
from jax.experimental.pallas import tpu as pltpu
from jax.sharding import PartitionSpec as P

HEADS = 16
MESH = pl.DeviceIdType.MESH
masked_score = -1e30


def layer_norm(values):
    center = values - jnp.mean(values, axis=-1, keepdims=True)
    spread = jnp.mean(center * center, axis=-1, keepdims=True)
    return center * lax.rsqrt(spread + 1e-06)


def time_modulation(timestep, time_weight):
    half_count = time_weight.shape[0] // 2
    rates = jnp.exp(-math.log(10000.0) * jnp.arange(half_count, dtype=jnp.float32) / half_count)
    angles = 1000.0 * timestep[0] * rates
    features = jnp.concatenate([jnp.cos(angles), jnp.sin(angles)])
    return jnp.dot(jax.nn.silu(features)[None, :], time_weight, precision=lax.Precision.HIGHEST)[0]


def project_kernel(
    dims,
    states_ref,
    proj_ref,
    mixed_ref,
    lift_ref,
    phase_ref,
    mod_ref,
    weight_ref,
    start_ref,
    kv_all,
    q_all,
    part_buf,
    got_buf,
    cond_buf,
    mix_buf,
    kv_buf,
    q_buf,
    part_send,
    part_recv,
    cond_send,
    cond_recv,
    mix_send,
    mix_recv,
    kv_send,
    kv_recv,
    q_send,
    q_recv,
):
    seq_n, tp_n, heads, ranks, dim, upsample = dims
    me = lax.axis_index("seq")
    tp = lax.axis_index("tp")
    tokens = cond_buf.shape[1]
    frames = mixed_ref.shape[0]
    cols = heads * dim

    barrier = pltpu.get_barrier_semaphore()
    for d in range(1, tp_n):
        pl.semaphore_signal(
            barrier, inc=1, device_id=(me, lax.rem(tp + d, tp_n)), device_id_type=MESH
        )
    for d in range(1, seq_n):
        pl.semaphore_signal(
            barrier, inc=1, device_id=(lax.rem(me + d, seq_n), tp), device_id_type=MESH
        )
    pl.semaphore_wait(barrier, tp_n - 1 + seq_n - 1)

    def tp_copy(src, dst, send, recv, d):
        return pltpu.make_async_remote_copy(
            src_ref=src,
            dst_ref=dst,
            send_sem=send.at[d],
            recv_sem=recv.at[d],
            device_id=(me, lax.rem(tp + d, tp_n)),
            device_id_type=MESH,
        )

    def mix_copy(d):
        return tp_copy(mixed_ref, mix_buf.at[d], mix_send, mix_recv, d)

    def part_copy(d):
        return tp_copy(part_buf.at[d], got_buf.at[d], part_send, part_recv, d)

    def cond_copy(d):
        return tp_copy(cond_buf.at[0], cond_buf.at[d], cond_send, cond_recv, d)

    for d in range(1, tp_n):
        mix_copy(d).start()
    mix_buf[0] = mixed_ref[...]
    own = None
    for d in list(range(1, tp_n)) + [0]:
        rows = pl.ds(pl.multiple_of(lax.rem(tp + d, tp_n) * tokens, tokens), tokens)
        piece = jnp.dot(states_ref[rows, :], proj_ref[...], preferred_element_type=jnp.float32)
        if d:
            part_buf[d] = piece.astype(jnp.bfloat16)
            part_copy(d).start()
        else:
            own = piece
    for d in range(1, tp_n):
        part_copy(d).wait_recv()
        own = own + got_buf[d].astype(jnp.float32)
    cond_buf[0] = own.astype(jnp.bfloat16)
    for d in range(1, tp_n):
        cond_copy(d).start()

    frame_at = lax.broadcasted_iota(jnp.int32, (frames, tokens), 0)
    first = lax.broadcasted_iota(jnp.int32, (frames, tokens), 1) * upsample
    spread = jnp.where((frame_at >= first) & (frame_at < first + upsample), 1.0, 0.0).astype(
        jnp.bfloat16
    )
    q_factor = math.log2(math.e) / math.sqrt(dim)

    def kv_copy(chunk, d):
        dest = lax.rem(me + d, seq_n)
        return pltpu.make_async_remote_copy(
            src_ref=kv_buf.at[chunk, dest // ranks],
            dst_ref=kv_all.at[me, chunk],
            send_sem=kv_send.at[d, chunk],
            recv_sem=kv_recv.at[d, chunk],
            device_id=(dest, tp),
            device_id_type=MESH,
        )

    def q_copy(chunk, d):
        dest = lax.rem(me + d, seq_n)
        return pltpu.make_async_remote_copy(
            src_ref=q_buf.at[chunk, dest // ranks],
            dst_ref=q_all.at[me, chunk // ranks],
            send_sem=q_send.at[d, chunk // ranks],
            recv_sem=q_recv.at[d, chunk // ranks],
            device_id=(dest, tp),
            device_id_type=MESH,
        )

    def own_kv(chunk):
        return pltpu.make_async_copy(
            kv_buf.at[chunk, me // ranks], kv_all.at[me, chunk], kv_send.at[0, chunk]
        )

    def own_q(chunk):
        return pltpu.make_async_copy(
            q_buf.at[chunk, me // ranks],
            q_all.at[me, chunk // ranks],
            q_send.at[0, chunk // ranks],
        )

    @pl.loop(0, tp_n)
    def _(step):
        chunk = lax.rem(tp - step + tp_n, tp_n)

        @pl.when(step > 0)
        def _():
            mix_copy(step).wait_recv()
            cond_copy(step).wait_recv()

        state = jnp.dot(mix_buf[step], lift_ref[...], preferred_element_type=jnp.float32)
        state = state + jnp.dot(spread, cond_buf[step], preferred_element_type=jnp.float32)
        state = (
            state.reshape(frames // 8, 8, state.shape[1]) + phase_ref[...][None]
        ).reshape(state.shape)

        @pl.when(step == 0)
        def _():
            start_ref[...] = state

        normed = (layer_norm(state) * mod_ref[1:2, :] + mod_ref[0:1, :]).astype(jnp.bfloat16)
        for kind in range(3):
            made = jnp.dot(
                normed,
                weight_ref[:, kind * cols : (kind + 1) * cols],
                preferred_element_type=jnp.float32,
            ).T
            if kind == 0:
                q_buf[chunk] = (made * q_factor).astype(jnp.bfloat16).reshape(heads, dim, frames)
            else:
                kv_buf[chunk, :, (kind - 1) * dim : kind * dim, :] = made.astype(
                    jnp.bfloat16
                ).reshape(heads, dim, frames)
        for d in range(1, seq_n):
            kv_copy(chunk, d).start()

            @pl.when(lax.rem(chunk, ranks) == lax.rem(lax.rem(me + d, seq_n), ranks))
            def _():
                q_copy(chunk, d).start()

        own_kv(chunk).start()

        @pl.when(lax.rem(chunk, ranks) == lax.rem(me, ranks))
        def _():
            own_q(chunk).start()

    for d in range(1, tp_n):
        mix_copy(d).wait_send()
        part_copy(d).wait_send()
        cond_copy(d).wait_send()
    for chunk in range(tp_n):
        own_kv(chunk).wait()
        for d in range(1, seq_n):
            kv_copy(chunk, d).wait()
    for k in range(tp_n // ranks):
        own_q(k * ranks).wait()
        for d in range(1, seq_n):
            q_copy(k * ranks, d).wait()


def attend_kernel(
    dims,
    natural_ref,
    place_ref,
    first_ref,
    ends_ref,
    q_ref,
    kv_ref,
    out_ref,
    key_buf,
    value_buf,
):
    seq_n, tp_n, dim, block_len = dims
    frames = q_ref.shape[-1]
    per_block = block_len // frames
    block_count = place_ref.shape[0]
    tile = pl.program_id(0)
    value_rows = value_buf.shape[1]

    @pl.when(tile == 0)
    def _():
        @pl.loop(0, seq_n * tp_n)
        def _(i):
            at = pl.ds(pl.multiple_of(i * frames, frames), frames)
            key_buf[at, :] = kv_ref[i, :dim, :].astype(jnp.float32).T.astype(jnp.bfloat16)
            value_buf[i, :dim, :] = kv_ref[i, dim:, :]
            value_buf[i, dim:, :] = jnp.ones((value_rows - dim, frames), jnp.bfloat16)

    queries = q_ref[0]
    natural = natural_ref[tile]
    base = natural * block_len
    at = first_ref[tile] + lax.broadcasted_iota(jnp.int32, (1, frames), 1)
    ends = ends_ref[...]
    stop = jnp.min(jnp.where(ends > at, ends, 1 << 30), axis=0, keepdims=True)

    def visit(carry, stored, count, limit):
        highest, total = carry
        keys = key_buf[pl.ds(pl.multiple_of(stored * block_len, block_len), count), :]
        scores = jnp.dot(keys, queries, preferred_element_type=jnp.float32)
        if limit is not None:
            row = lax.broadcasted_iota(jnp.int32, (count, frames), 0)
            scores = jnp.where(row < limit, scores, masked_score)
        above = jnp.maximum(highest, jnp.max(scores, axis=0, keepdims=True))
        expo = jnp.exp2(scores - above).astype(jnp.bfloat16)
        total = total * jnp.exp2(highest - above)
        for c in range(pl.cdiv(count, frames)):
            size = min(frames, count - c * frames)
            total = total + jnp.dot(
                value_buf[stored * per_block + c, :, :size],
                expo[c * frames : c * frames + size],
                preferred_element_type=jnp.float32,
            )
        return above, total

    carry = (
        jnp.full((1, frames), masked_score, jnp.float32),
        jnp.zeros((value_rows, frames), jnp.float32),
    )
    carry = visit(carry, place_ref[natural], block_len, stop - base)
    beyond = jnp.minimum(natural + 1, block_count - 1)
    carry = visit(
        carry,
        place_ref[beyond],
        128,
        jnp.where(natural + 1 < block_count, stop - base - block_len, 0),
    )

    def pair(i, carry):
        carry = visit(carry, place_ref[2 * i], block_len, None)
        return visit(carry, place_ref[2 * i + 1], block_len, None)

    carry = lax.fori_loop(0, natural // 2, pair, carry)
    carry = lax.fori_loop(
        2 * (natural // 2),
        natural,
        lambda j, carry: visit(carry, place_ref[j], block_len, None),
        carry,
    )
    total = carry[1]
    out_ref[0] = (total[:dim] / total[dim : dim + 1]).astype(jnp.bfloat16)


def return_kernel(dims, att_ref, out_ref, send_sem, recv_sem):
    seq_n, tp_n, heads, ranks = dims
    me = lax.axis_index("seq")
    tp = lax.axis_index("tp")
    rank = lax.rem(me, ranks)
    per = tp_n // ranks

    barrier = pltpu.get_barrier_semaphore()

    for p in range(heads):
        for t in range(tp_n):
            other = p * ranks + lax.rem(tp, ranks)

            @pl.when((other != me) | (t != tp))
            def _():
                pl.semaphore_signal(barrier, inc=1, device_id=(other, t), device_id_type=MESH)

    pl.semaphore_wait(barrier, seq_n * per - jnp.where(lax.rem(tp, ranks) == rank, 1, 0))

    mine = tp * heads + me // ranks

    def copy(i, k):
        s = lax.rem(me + i, seq_n)
        return pltpu.make_async_remote_copy(
            src_ref=att_ref.at[s, k],
            dst_ref=out_ref.at[mine],
            send_sem=send_sem.at[i, k],
            recv_sem=recv_sem.at[mine],
            device_id=(s, k * ranks + rank),
            device_id_type=MESH,
        )

    def local(k):
        return pltpu.make_async_copy(att_ref.at[me, k], out_ref.at[mine], send_sem.at[0, k])

    for i in range(seq_n):
        for k in range(per):
            if i:
                copy(i, k).start()
            else:

                @pl.when(k * ranks + rank != tp)
                def _():
                    copy(0, k).start()

                @pl.when(k * ranks + rank == tp)
                def _():
                    local(k).start()

    for i in range(seq_n):
        for k in range(per):
            if i:
                copy(i, k).wait_send()
            else:

                @pl.when(k * ranks + rank != tp)
                def _():
                    copy(0, k).wait_send()

                @pl.when(k * ranks + rank == tp)
                def _():
                    local(k).wait()

    for t in range(tp_n):
        for p in range(heads):
            source = p * ranks + lax.rem(tp, ranks)

            @pl.when((source != me) | (t != tp))
            def _():
                pltpu.make_async_remote_copy(
                    src_ref=att_ref.at[0, 0],
                    dst_ref=out_ref.at[t * heads + p],
                    send_sem=send_sem.at[0, 0],
                    recv_sem=recv_sem.at[t * heads + p],
                    device_id=(source, t),
                    device_id_type=MESH,
                ).wait_recv()


def body(
    semantic_states,
    token_projection,
    phase_offsets,
    target_spectrum,
    noise,
    timestep,
    frame_lift,
    time_weight,
    attention_weight,
    head_mixing,
    velocity_head,
    group_index,
    block_order,
):
    width = token_projection.shape[1]
    frame_count, bins = target_spectrum.shape
    upsample = phase_offsets.shape[0]
    tp_n = lax.axis_size("tp")
    seq_n = lax.axis_size("seq")
    cols = attention_weight.shape[2]
    dim = width // HEADS
    heads = cols // dim
    ranks = seq_n // heads
    per = tp_n // ranks
    tokens = semantic_states.shape[0] // tp_n
    frames_total = group_index.shape[0]
    block_count = block_order.shape[0]
    block_len = frames_total // block_count
    frames_dev = frame_count * tp_n
    blocks_dev = frames_dev // block_len
    me = lax.axis_index("seq")

    moment = timestep[0]
    mixed = ((1.0 - moment) * noise + moment * target_spectrum).astype(jnp.bfloat16)
    padding = -bins % 128
    mixed = jnp.pad(mixed, ((0, 0), (0, padding)))
    lift = jnp.pad(frame_lift, ((0, padding), (0, 0)))
    modulation = time_modulation(timestep, time_weight)
    mod = jnp.stack([modulation[:width], 1.0 + modulation[width:]])
    phase = jnp.tile(phase_offsets, (8 // upsample, 1))
    mixing = lax.all_gather(head_mixing, "tp", axis=0, tiled=True)

    vmem = pl.BlockSpec(memory_space=pltpu.VMEM)
    hbm = pl.BlockSpec(memory_space=pl.ANY)
    dma = pltpu.SemaphoreType.DMA
    bf16 = jnp.bfloat16
    start_state, kv_all, q_all = pl.pallas_call(
        functools.partial(project_kernel, (seq_n, tp_n, heads, ranks, dim, upsample)),
        out_shape=(
            jax.ShapeDtypeStruct((frame_count, width), jnp.float32),
            jax.ShapeDtypeStruct((seq_n, tp_n, 2 * dim, frame_count), bf16),
            jax.ShapeDtypeStruct((seq_n, per, dim, frame_count), bf16),
        ),
        in_specs=[vmem] * 7,
        out_specs=(vmem, hbm, hbm),
        scratch_shapes=[
            pltpu.VMEM((tp_n, tokens, width), bf16),
            pltpu.VMEM((tp_n, tokens, width), bf16),
            pltpu.VMEM((tp_n, tokens, width), bf16),
            pltpu.VMEM((tp_n, frame_count, bins + padding), bf16),
            pltpu.VMEM((tp_n, heads, 2 * dim, frame_count), bf16),
            pltpu.VMEM((tp_n, heads, dim, frame_count), bf16),
        ]
        + [dma((tp_n,))] * 6
        + [dma((seq_n, tp_n))] * 2
        + [dma((seq_n, per))] * 2,
        compiler_params=pltpu.CompilerParams(
            collective_id=0, has_side_effects=True, vmem_limit_bytes=40 << 20
        ),
        name="project",
    )(
        semantic_states,
        token_projection,
        mixed,
        lift,
        phase,
        mod,
        attention_weight.reshape(width, 3 * cols),
    )

    group_ids = jnp.arange(frames_total // 64, dtype=jnp.int32)
    ends = jnp.sum((group_index[None, :] <= group_ids[:, None]).astype(jnp.int32), axis=1)[:, None]
    blocks = jnp.arange(block_count, dtype=jnp.int32)
    place = jnp.sum(
        jnp.where(block_order[None, :] == blocks[:, None], blocks[None, :], 0), axis=1
    ).astype(jnp.int32)
    owner = jnp.arange(per, dtype=jnp.int32) * ranks + me % ranks
    stored = (
        jnp.arange(seq_n, dtype=jnp.int32)[:, None] * blocks_dev
        + (owner * frame_count // block_len)[None, :]
    ).reshape(-1)
    natural = jnp.sum(
        jnp.where(stored[:, None] == blocks[None, :], block_order[None, :], 0), axis=1
    ).astype(jnp.int32)
    first = natural * block_len + jnp.tile(owner * frame_count % block_len, seq_n)

    tiles = seq_n * per
    attended = pl.pallas_call(
        functools.partial(attend_kernel, (seq_n, tp_n, dim, block_len)),
        out_shape=jax.ShapeDtypeStruct((tiles, dim, frame_count), bf16),
        grid_spec=pltpu.PrefetchScalarGridSpec(
            num_scalar_prefetch=3,
            grid=(tiles,),
            in_specs=[
                vmem,
                pl.BlockSpec((1, dim, frame_count), lambda i, *_: (i, 0, 0)),
                vmem,
            ],
            out_specs=pl.BlockSpec((1, dim, frame_count), lambda i, *_: (i, 0, 0)),
            scratch_shapes=[
                pltpu.VMEM((frames_total, dim), bf16),
                pltpu.VMEM((seq_n * tp_n, dim + 16, frame_count), bf16),
            ],
        ),
        compiler_params=pltpu.CompilerParams(vmem_limit_bytes=40 << 20),
        name="attend",
    )(
        natural,
        place,
        first,
        ends,
        q_all.reshape(tiles, dim, frame_count),
        kv_all.reshape(seq_n * tp_n, 2 * dim, frame_count),
    )

    gathered = pl.pallas_call(
        functools.partial(return_kernel, (seq_n, tp_n, heads, ranks)),
        out_shape=jax.ShapeDtypeStruct((HEADS, dim, frame_count), bf16),
        in_specs=[hbm],
        out_specs=hbm,
        scratch_shapes=[dma((seq_n, per)), dma((HEADS,))],
        compiler_params=pltpu.CompilerParams(collective_id=1, has_side_effects=True),
        name="give_back",
    )(attended.reshape(seq_n, per, dim, frame_count))

    update = lax.dot_general(
        gathered.reshape(width, frame_count),
        mixing,
        (((0,), (0,)), ((), ())),
        preferred_element_type=jnp.float32,
    )
    closing = layer_norm(start_state + update).astype(jnp.bfloat16)
    return jnp.dot(closing, velocity_head, preferred_element_type=jnp.float32)


def solution(mesh):
    in_specs = (
        P("seq", "tp"),
        P("tp", None),
        P(),
        P(("seq", "tp"), None),
        P(("seq", "tp"), None),
        P(),
        P(),
        P(),
        P(None, None, "tp"),
        P("tp", None),
        P(),
        P(),
        P(),
    )
    out_specs = P(("seq", "tp"), None)
    return jax.shard_map(body, mesh=mesh, in_specs=in_specs, out_specs=out_specs, check_vma=False)
```

```python
import functools
import math

import jax
import jax.numpy as jnp
from jax import lax
from jax.experimental import pallas as pl
from jax.experimental.pallas import tpu as pltpu
from jax.sharding import PartitionSpec as P

HEADS = 16
MESH = pl.DeviceIdType.MESH
masked_score = -1e30


def layer_norm(values):
    center = values - jnp.mean(values, axis=-1, keepdims=True)
    spread = jnp.mean(center * center, axis=-1, keepdims=True)
    return center * lax.rsqrt(spread + 1e-06)


def time_modulation(timestep, time_weight):
    half_count = time_weight.shape[0] // 2
    rates = jnp.exp(-math.log(10000.0) * jnp.arange(half_count, dtype=jnp.float32) / half_count)
    angles = 1000.0 * timestep[0] * rates
    features = jnp.concatenate([jnp.cos(angles), jnp.sin(angles)])
    return jnp.dot(jax.nn.silu(features)[None, :], time_weight, precision=lax.Precision.HIGHEST)[0]


def project_kernel(
    dims,
    states_ref,
    proj_ref,
    mixed_ref,
    lift_ref,
    phase_ref,
    mod_ref,
    weight_ref,
    start_ref,
    kv_all,
    q_all,
    part_buf,
    got_buf,
    cond_buf,
    mix_buf,
    kv_buf,
    q_buf,
    part_send,
    part_recv,
    cond_send,
    cond_recv,
    mix_send,
    mix_recv,
    kv_send,
    kv_recv,
    q_send,
    q_recv,
):
    seq_n, tp_n, heads, ranks, dim, upsample = dims
    me = lax.axis_index("seq")
    tp = lax.axis_index("tp")
    tokens = cond_buf.shape[1]
    frames = mixed_ref.shape[1]

    barrier = pltpu.get_barrier_semaphore()
    for d in range(1, tp_n):
        pl.semaphore_signal(
            barrier, inc=1, device_id=(me, lax.rem(tp + d, tp_n)), device_id_type=MESH
        )
    for d in range(1, seq_n):
        pl.semaphore_signal(
            barrier, inc=1, device_id=(lax.rem(me + d, seq_n), tp), device_id_type=MESH
        )
    pl.semaphore_wait(barrier, tp_n - 1 + seq_n - 1)

    def tp_copy(src, dst, send, recv, d):
        return pltpu.make_async_remote_copy(
            src_ref=src,
            dst_ref=dst,
            send_sem=send.at[d],
            recv_sem=recv.at[d],
            device_id=(me, lax.rem(tp + d, tp_n)),
            device_id_type=MESH,
        )

    def mix_copy(d):
        return tp_copy(mixed_ref, mix_buf.at[d], mix_send, mix_recv, d)

    def part_copy(d):
        return tp_copy(part_buf.at[d], got_buf.at[d], part_send, part_recv, d)

    def cond_copy(d):
        return tp_copy(cond_buf.at[0], cond_buf.at[d], cond_send, cond_recv, d)

    for d in range(1, tp_n):
        mix_copy(d).start()
    mix_buf[0] = mixed_ref[...]
    own = None
    for d in list(range(1, tp_n)) + [0]:
        rows = pl.ds(pl.multiple_of(lax.rem(tp + d, tp_n) * tokens, tokens), tokens)
        piece = jnp.dot(states_ref[rows, :], proj_ref[...], preferred_element_type=jnp.float32)
        if d:
            part_buf[d] = piece.astype(jnp.bfloat16)
            part_copy(d).start()
        else:
            own = piece
    for d in range(1, tp_n):
        part_copy(d).wait_recv()
        own = own + got_buf[d].astype(jnp.float32)
    cond_buf[0] = own.astype(jnp.bfloat16)
    for d in range(1, tp_n):
        cond_copy(d).start()

    frame_at = lax.broadcasted_iota(jnp.int32, (frames, tokens), 0)
    first = lax.broadcasted_iota(jnp.int32, (frames, tokens), 1) * upsample
    spread = jnp.where((frame_at >= first) & (frame_at < first + upsample), 1.0, 0.0).astype(
        jnp.bfloat16
    )
    phase = jnp.concatenate([phase_ref[...]] * (8 // upsample), axis=0)
    q_factor = math.log2(math.e) / math.sqrt(dim)

    def kv_copy(chunk, d):
        dest = lax.rem(me + d, seq_n)
        return pltpu.make_async_remote_copy(
            src_ref=kv_buf.at[chunk, dest // ranks],
            dst_ref=kv_all.at[me, chunk],
            send_sem=kv_send.at[d, chunk],
            recv_sem=kv_recv.at[d, chunk],
            device_id=(dest, tp),
            device_id_type=MESH,
        )

    def q_copy(chunk, d):
        dest = lax.rem(me + d, seq_n)
        return pltpu.make_async_remote_copy(
            src_ref=q_buf.at[chunk, dest // ranks],
            dst_ref=q_all.at[me, chunk // ranks],
            send_sem=q_send.at[d, chunk // ranks],
            recv_sem=q_recv.at[d, chunk // ranks],
            device_id=(dest, tp),
            device_id_type=MESH,
        )

    def own_kv(chunk):
        return pltpu.make_async_copy(
            kv_buf.at[chunk, me // ranks], kv_all.at[me, chunk], kv_send.at[0, chunk]
        )

    def own_q(chunk):
        return pltpu.make_async_copy(
            q_buf.at[chunk, me // ranks],
            q_all.at[me, chunk // ranks],
            q_send.at[0, chunk // ranks],
        )

    @pl.loop(0, tp_n)
    def _(step):
        chunk = lax.rem(tp - step + tp_n, tp_n)

        @pl.when(step > 0)
        def _():
            mix_copy(step).wait_recv()
            cond_copy(step).wait_recv()

        state = lax.dot_general(
            mix_buf[step],
            lift_ref[...],
            (((0,), (0,)), ((), ())),
            preferred_element_type=jnp.float32,
        )
        state = state + jnp.dot(spread, cond_buf[step], preferred_element_type=jnp.float32)
        state = (state.reshape(frames // 8, 8, state.shape[1]) + phase[None]).reshape(state.shape)

        @pl.when(step == 0)
        def _():
            start_ref[...] = state

        normed = (layer_norm(state) * mod_ref[1:2, :] + mod_ref[0:1, :]).astype(jnp.bfloat16)
        for kind in range(3):
            made = jnp.dot(
                normed,
                weight_ref[kind],
                preferred_element_type=jnp.float32,
            ).T
            if kind == 0:
                q_buf[chunk] = (made * q_factor).astype(jnp.bfloat16).reshape(heads, dim, frames)
            else:
                kv_buf[chunk, :, (kind - 1) * dim : kind * dim, :] = made.astype(
                    jnp.bfloat16
                ).reshape(heads, dim, frames)
        for d in range(1, seq_n):
            kv_copy(chunk, d).start()

            @pl.when(lax.rem(chunk, ranks) == lax.rem(lax.rem(me + d, seq_n), ranks))
            def _():
                q_copy(chunk, d).start()

        own_kv(chunk).start()

        @pl.when(lax.rem(chunk, ranks) == lax.rem(me, ranks))
        def _():
            own_q(chunk).start()

    for d in range(1, tp_n):
        mix_copy(d).wait_send()
        part_copy(d).wait_send()
        cond_copy(d).wait_send()
    for chunk in range(tp_n):
        own_kv(chunk).wait()
        for d in range(1, seq_n):
            kv_copy(chunk, d).wait()
    for k in range(tp_n // ranks):
        own_q(k * ranks).wait()
        for d in range(1, seq_n):
            q_copy(k * ranks, d).wait()


def attend_kernel(
    dims,
    natural_ref,
    place_ref,
    first_ref,
    ends_ref,
    q_ref,
    kv_ref,
    out_ref,
    key_buf,
    value_buf,
    even_buf,
    odd_buf,
):
    seq_n, tp_n, dim, block_len = dims
    frames = q_ref.shape[-1]
    per_block = block_len // frames
    block_count = place_ref.shape[0]
    tile = pl.program_id(0)
    value_rows = value_buf.shape[1]

    @pl.when(tile == 0)
    def _():
        @pl.loop(0, seq_n * tp_n)
        def _(i):
            at = pl.ds(pl.multiple_of(i * frames, frames), frames)
            key_buf[at, :] = kv_ref[i, :dim, :].astype(jnp.float32).T.astype(jnp.bfloat16)
            value_buf[i, :dim, :] = kv_ref[i, dim:, :]
            value_buf[i, dim:, :] = jnp.ones((value_rows - dim, frames), jnp.bfloat16)

    queries = q_ref[0]
    natural = natural_ref[tile]
    base = natural * block_len
    at = first_ref[tile] + lax.broadcasted_iota(jnp.int32, (1, frames), 1)
    ends = ends_ref[...]
    stop = jnp.min(jnp.where(ends > at, ends, 1 << 30), axis=0, keepdims=True)

    def score(stored, count):
        keys = key_buf[pl.ds(pl.multiple_of(stored * block_len, block_len), count), :]
        return jnp.dot(keys, queries, preferred_element_type=jnp.float32)

    def absorb(carry, *parts):
        highest, total = carry
        above = highest
        for scores, _ in parts:
            above = jnp.maximum(above, jnp.max(scores, axis=0, keepdims=True))
        total = total * jnp.exp2(highest - above)
        for scores, stored in parts:
            count = scores.shape[0]
            expo = jnp.exp2((scores - above)).astype(jnp.bfloat16)
            for c in range(pl.cdiv(count, frames)):
                size = min(frames, count - c * frames)
                total = total + jnp.dot(
                    value_buf[stored * per_block + c, :, :size],
                    expo[c * frames : c * frames + size],
                    preferred_element_type=jnp.float32,
                )
        return above, total

    def masked(scores, limit):
        row = lax.broadcasted_iota(jnp.int32, scores.shape, 0)
        return jnp.where(row < limit, scores, masked_score)

    carry = (
        jnp.full((1, frames), masked_score, jnp.float32),
        jnp.zeros((value_rows, frames), jnp.float32),
    )
    here = place_ref[natural]
    beyond = place_ref[jnp.minimum(natural + 1, block_count - 1)]
    over = jnp.where(natural + 1 < block_count, stop - base - block_len, 0)
    here_scores = score(here, block_len)
    beyond_scores = score(beyond, 128)
    even_buf[...] = score(place_ref[0], block_len)
    carry = absorb(
        carry, (masked(here_scores, stop - base), here), (masked(beyond_scores, over), beyond)
    )

    def pair(i, carry):
        odd_buf[...] = score(place_ref[2 * i + 1], block_len)
        carry = absorb(carry, (even_buf[...], place_ref[2 * i]))
        even_buf[...] = score(place_ref[2 * i + 2], block_len)
        return absorb(carry, (odd_buf[...], place_ref[2 * i + 1]))

    carry = lax.fori_loop(0, natural // 2, pair, carry)
    last = natural - lax.rem(natural, 2)
    carry = lax.fori_loop(
        last, natural, lambda j, carry: absorb(carry, (even_buf[...], place_ref[j])), carry
    )
    total = carry[1]
    out_ref[0] = (total[:dim] / total[dim : dim + 1]).astype(jnp.bfloat16)


def attend_call(dims, natural, place, first, ends, queries, keys_values):
    block_len = dims[3]
    tiles, dim, frames = queries.shape
    chunks = keys_values.shape[0]
    scores = pltpu.VMEM((block_len, frames), jnp.float32)
    return pl.pallas_call(
        functools.partial(attend_kernel, dims),
        out_shape=jax.ShapeDtypeStruct((tiles, dim, frames), jnp.bfloat16),
        grid_spec=pltpu.PrefetchScalarGridSpec(
            num_scalar_prefetch=3,
            grid=(tiles,),
            in_specs=[
                pl.BlockSpec(memory_space=pltpu.VMEM),
                pl.BlockSpec((1, dim, frames), lambda i, *_: (i, 0, 0)),
                pl.BlockSpec(memory_space=pltpu.VMEM),
            ],
            out_specs=pl.BlockSpec((1, dim, frames), lambda i, *_: (i, 0, 0)),
            scratch_shapes=[
                pltpu.VMEM((chunks * frames, dim), jnp.bfloat16),
                pltpu.VMEM((chunks, dim + 16, frames), jnp.bfloat16),
                scores,
                scores,
            ],
        ),
        compiler_params=pltpu.CompilerParams(vmem_limit_bytes=40 << 20),
        name="attend",
    )(natural, place, first, ends, queries, keys_values)


def return_kernel(dims, att_ref, out_ref, send_sem, recv_sem):
    seq_n, tp_n, heads, ranks = dims
    me = lax.axis_index("seq")
    tp = lax.axis_index("tp")
    rank = lax.rem(me, ranks)
    per = tp_n // ranks

    barrier = pltpu.get_barrier_semaphore()

    for p in range(heads):
        for t in range(tp_n):
            other = p * ranks + lax.rem(tp, ranks)

            @pl.when((other != me) | (t != tp))
            def _():
                pl.semaphore_signal(barrier, inc=1, device_id=(other, t), device_id_type=MESH)

    pl.semaphore_wait(barrier, seq_n * per - jnp.where(lax.rem(tp, ranks) == rank, 1, 0))

    mine = tp * heads + me // ranks

    def copy(i, k):
        s = lax.rem(me + i, seq_n)
        return pltpu.make_async_remote_copy(
            src_ref=att_ref.at[s, k],
            dst_ref=out_ref.at[mine],
            send_sem=send_sem.at[i, k],
            recv_sem=recv_sem.at[mine],
            device_id=(s, k * ranks + rank),
            device_id_type=MESH,
        )

    def local(k):
        return pltpu.make_async_copy(att_ref.at[me, k], out_ref.at[mine], send_sem.at[0, k])

    for i in range(seq_n):
        for k in range(per):
            if i:
                copy(i, k).start()
            else:

                @pl.when(k * ranks + rank != tp)
                def _():
                    copy(0, k).start()

                @pl.when(k * ranks + rank == tp)
                def _():
                    local(k).start()

    for i in range(seq_n):
        for k in range(per):
            if i:
                copy(i, k).wait_send()
            else:

                @pl.when(k * ranks + rank != tp)
                def _():
                    copy(0, k).wait_send()

                @pl.when(k * ranks + rank == tp)
                def _():
                    local(k).wait()

    for t in range(tp_n):
        for p in range(heads):
            source = p * ranks + lax.rem(tp, ranks)

            @pl.when((source != me) | (t != tp))
            def _():
                pltpu.make_async_remote_copy(
                    src_ref=att_ref.at[0, 0],
                    dst_ref=out_ref.at[t * heads + p],
                    send_sem=send_sem.at[0, 0],
                    recv_sem=recv_sem.at[t * heads + p],
                    device_id=(source, t),
                    device_id_type=MESH,
                ).wait_recv()


def body(
    semantic_states,
    token_projection,
    phase_offsets,
    target_spectrum,
    noise,
    timestep,
    frame_lift,
    time_weight,
    attention_weight,
    head_mixing,
    velocity_head,
    group_index,
    block_order,
):
    width = token_projection.shape[1]
    frame_count, bins = target_spectrum.shape
    upsample = phase_offsets.shape[0]
    tp_n = lax.axis_size("tp")
    seq_n = lax.axis_size("seq")
    cols = attention_weight.shape[2]
    dim = width // HEADS
    heads = cols // dim
    ranks = seq_n // heads
    per = tp_n // ranks
    tokens = semantic_states.shape[0] // tp_n
    frames_total = group_index.shape[0]
    block_count = block_order.shape[0]
    block_len = frames_total // block_count
    frames_dev = frame_count * tp_n
    blocks_dev = frames_dev // block_len
    me = lax.axis_index("seq")

    moment = timestep[0]
    mixed = ((1.0 - moment) * noise.T + moment * target_spectrum.T).astype(jnp.bfloat16)
    modulation = time_modulation(timestep, time_weight)
    mod = jnp.stack([modulation[:width], 1.0 + modulation[width:]])

    vmem = pl.BlockSpec(memory_space=pltpu.VMEM)
    hbm = pl.BlockSpec(memory_space=pl.ANY)
    dma = pltpu.SemaphoreType.DMA
    bf16 = jnp.bfloat16
    start_state, kv_all, q_all = pl.pallas_call(
        functools.partial(project_kernel, (seq_n, tp_n, heads, ranks, dim, upsample)),
        out_shape=(
            jax.ShapeDtypeStruct((frame_count, width), jnp.float32),
            jax.ShapeDtypeStruct((seq_n, tp_n, 2 * dim, frame_count), bf16),
            jax.ShapeDtypeStruct((seq_n, per, dim, frame_count), bf16),
        ),
        in_specs=[vmem] * 7,
        out_specs=(vmem, hbm, hbm),
        scratch_shapes=[
            pltpu.VMEM((tp_n, tokens, width), bf16),
            pltpu.VMEM((tp_n, tokens, width), bf16),
            pltpu.VMEM((tp_n, tokens, width), bf16),
            pltpu.VMEM((tp_n, bins, frame_count), bf16),
            pltpu.VMEM((tp_n, heads, 2 * dim, frame_count), bf16),
            pltpu.VMEM((tp_n, heads, dim, frame_count), bf16),
        ]
        + [dma((tp_n,))] * 6
        + [dma((seq_n, tp_n))] * 2
        + [dma((seq_n, per))] * 2,
        compiler_params=pltpu.CompilerParams(
            collective_id=0, has_side_effects=True, vmem_limit_bytes=40 << 20
        ),
        name="project",
    )(
        semantic_states,
        token_projection,
        mixed,
        frame_lift,
        phase_offsets,
        mod,
        attention_weight.transpose(1, 0, 2),
    )

    head_mixing, q_all = lax.optimization_barrier((head_mixing, q_all))
    mixing = lax.all_gather(head_mixing, "tp", axis=0, tiled=True)

    group_ids = jnp.arange(frames_total // 64, dtype=jnp.int32)
    ends = jnp.sum((group_index[None, :] <= group_ids[:, None]).astype(jnp.int32), axis=1)[:, None]
    blocks = jnp.arange(block_count, dtype=jnp.int32)
    place = jnp.sum(
        jnp.where(block_order[None, :] == blocks[:, None], blocks[None, :], 0), axis=1
    ).astype(jnp.int32)
    owner = jnp.arange(per, dtype=jnp.int32) * ranks + me % ranks
    stored = (
        jnp.arange(seq_n, dtype=jnp.int32)[:, None] * blocks_dev
        + (owner * frame_count // block_len)[None, :]
    ).reshape(-1)
    natural = jnp.sum(
        jnp.where(stored[:, None] == blocks[None, :], block_order[None, :], 0), axis=1
    ).astype(jnp.int32)
    first = natural * block_len + jnp.tile(owner * frame_count % block_len, seq_n)

    tiles = seq_n * per
    attended = attend_call(
        (seq_n, tp_n, dim, block_len),
        natural,
        place,
        first,
        ends,
        q_all.reshape(tiles, dim, frame_count),
        kv_all.reshape(seq_n * tp_n, 2 * dim, frame_count),
    )

    gathered = pl.pallas_call(
        functools.partial(return_kernel, (seq_n, tp_n, heads, ranks)),
        out_shape=jax.ShapeDtypeStruct((HEADS, dim, frame_count), bf16),
        in_specs=[hbm],
        out_specs=hbm,
        scratch_shapes=[dma((seq_n, per)), dma((HEADS,))],
        compiler_params=pltpu.CompilerParams(collective_id=1, has_side_effects=True),
        name="give_back",
    )(attended.reshape(seq_n, per, dim, frame_count))

    update = lax.dot_general(
        gathered.reshape(width, frame_count),
        mixing,
        (((0,), (0,)), ((), ())),
        preferred_element_type=jnp.float32,
    )
    closing = layer_norm(start_state + update).astype(jnp.bfloat16)
    return jnp.dot(closing, velocity_head, preferred_element_type=jnp.float32)


def solution(mesh):
    in_specs = (
        P("seq", "tp"),
        P("tp", None),
        P(),
        P(("seq", "tp"), None),
        P(("seq", "tp"), None),
        P(),
        P(),
        P(),
        P(None, None, "tp"),
        P("tp", None),
        P(),
        P(),
        P(),
    )
    out_specs = P(("seq", "tp"), None)
    return jax.shard_map(body, mesh=mesh, in_specs=in_specs, out_specs=out_specs, check_vma=False)
```

```python
import functools
import math

import jax
import jax.numpy as jnp
from jax import lax
from jax.experimental import pallas as pl
from jax.experimental.pallas import tpu as pltpu
from jax.sharding import PartitionSpec as P

HEADS = 16
MESH = pl.DeviceIdType.MESH
masked_score = -1e30


def layer_norm(values):
    center = values - jnp.mean(values, axis=-1, keepdims=True)
    spread = jnp.mean(center * center, axis=-1, keepdims=True)
    return center * lax.rsqrt(spread + 1e-06)


def time_modulation(timestep, time_weight):
    half_count = time_weight.shape[0] // 2
    rates = jnp.exp(-math.log(10000.0) * jnp.arange(half_count, dtype=jnp.float32) / half_count)
    angles = 1000.0 * timestep[0] * rates
    features = jnp.concatenate([jnp.cos(angles), jnp.sin(angles)])
    return jnp.dot(jax.nn.silu(features)[None, :], time_weight, precision=lax.Precision.HIGHEST)[0]


def project_kernel(
    dims,
    states_ref,
    proj_ref,
    mixed_ref,
    lift_ref,
    phase_ref,
    mod_ref,
    weight_ref,
    start_ref,
    kv_all,
    q_all,
    part_buf,
    got_buf,
    cond_buf,
    mix_buf,
    kv_buf,
    q_buf,
    part_send,
    part_recv,
    cond_send,
    cond_recv,
    mix_send,
    mix_recv,
    kv_send,
    kv_recv,
    share_send,
    share_recv,
    q_send,
    q_recv,
):
    seq_n, tp_n, heads, ranks, dim, upsample = dims
    me = lax.axis_index("seq")
    tp = lax.axis_index("tp")
    tokens = cond_buf.shape[1]
    frames = mixed_ref.shape[1]

    barrier = pltpu.get_barrier_semaphore()
    for d in range(1, tp_n):
        pl.semaphore_signal(
            barrier, inc=1, device_id=(me, lax.rem(tp + d, tp_n)), device_id_type=MESH
        )
    for d in range(1, seq_n):
        pl.semaphore_signal(
            barrier, inc=1, device_id=(lax.rem(me + d, seq_n), tp), device_id_type=MESH
        )
    pl.semaphore_wait(barrier, tp_n - 1 + seq_n - 1)

    def tp_copy(src, dst, send, recv, d):
        return pltpu.make_async_remote_copy(
            src_ref=src,
            dst_ref=dst,
            send_sem=send.at[d],
            recv_sem=recv.at[d],
            device_id=(me, lax.rem(tp + d, tp_n)),
            device_id_type=MESH,
        )

    def mix_copy(d):
        return tp_copy(mixed_ref, mix_buf.at[d], mix_send, mix_recv, d)

    def part_copy(d):
        return tp_copy(part_buf.at[d], got_buf.at[d], part_send, part_recv, d)

    def cond_copy(d):
        return tp_copy(cond_buf.at[0], cond_buf.at[d], cond_send, cond_recv, d)

    for d in range(1, tp_n):
        mix_copy(d).start()
    mix_buf[0] = mixed_ref[...]
    own = None
    for d in list(range(1, tp_n)) + [0]:
        rows = pl.ds(pl.multiple_of(lax.rem(tp + d, tp_n) * tokens, tokens), tokens)
        piece = jnp.dot(states_ref[rows, :], proj_ref[...], preferred_element_type=jnp.float32)
        if d:
            part_buf[d] = piece.astype(jnp.bfloat16)
            part_copy(d).start()
        else:
            own = piece
    for d in range(1, tp_n):
        part_copy(d).wait_recv()
        own = own + got_buf[d].astype(jnp.float32)
    cond_buf[0] = own.astype(jnp.bfloat16)
    for d in range(1, tp_n):
        cond_copy(d).start()

    frame_at = lax.broadcasted_iota(jnp.int32, (frames, tokens), 0)
    first = lax.broadcasted_iota(jnp.int32, (frames, tokens), 1) * upsample
    spread = jnp.where((frame_at >= first) & (frame_at < first + upsample), 1.0, 0.0).astype(
        jnp.bfloat16
    )
    phase = jnp.concatenate([phase_ref[...]] * (8 // upsample), axis=0)
    q_factor = math.log2(math.e) / math.sqrt(dim)

    head = me // ranks
    rank = lax.rem(me, ranks)

    def kv_copy(chunk, d):
        goal = lax.rem(head + d, heads)
        return pltpu.make_async_remote_copy(
            src_ref=kv_buf.at[chunk, goal],
            dst_ref=kv_all.at[me, chunk],
            send_sem=kv_send.at[d, chunk],
            recv_sem=kv_recv.at[d, chunk],
            device_id=(goal * ranks + rank, tp),
            device_id_type=MESH,
        )

    def share_copy(chunk, d, j):
        source = lax.rem(head - d + heads, heads) * ranks + rank
        return pltpu.make_async_remote_copy(
            src_ref=kv_all.at[source, chunk] if d else kv_buf.at[chunk, head],
            dst_ref=kv_all.at[source, chunk],
            send_sem=share_send.at[d * ranks + j, chunk],
            recv_sem=share_recv.at[d * ranks + j, chunk],
            device_id=(head * ranks + lax.rem(rank + j, ranks), tp),
            device_id_type=MESH,
        )

    def q_copy(chunk, d):
        dest = lax.rem(me + d, seq_n)
        return pltpu.make_async_remote_copy(
            src_ref=q_buf.at[chunk, dest // ranks],
            dst_ref=q_all.at[me, chunk // ranks],
            send_sem=q_send.at[d, chunk // ranks],
            recv_sem=q_recv.at[d, chunk // ranks],
            device_id=(dest, tp),
            device_id_type=MESH,
        )

    def own_kv(chunk):
        return pltpu.make_async_copy(
            kv_buf.at[chunk, me // ranks], kv_all.at[me, chunk], kv_send.at[0, chunk]
        )

    def own_q(chunk):
        return pltpu.make_async_copy(
            q_buf.at[chunk, me // ranks],
            q_all.at[me, chunk // ranks],
            q_send.at[0, chunk // ranks],
        )

    @pl.loop(0, tp_n)
    def _(step):
        chunk = lax.rem(tp - step + tp_n, tp_n)

        @pl.when(step > 0)
        def _():
            mix_copy(step).wait_recv()
            cond_copy(step).wait_recv()

        state = lax.dot_general(
            mix_buf[step],
            lift_ref[...],
            (((0,), (0,)), ((), ())),
            preferred_element_type=jnp.float32,
        )
        state = state + jnp.dot(spread, cond_buf[step], preferred_element_type=jnp.float32)
        state = (state.reshape(frames // 8, 8, state.shape[1]) + phase[None]).reshape(state.shape)

        @pl.when(step == 0)
        def _():
            start_ref[...] = state

        normed = (layer_norm(state) * mod_ref[1:2, :] + mod_ref[0:1, :]).astype(jnp.bfloat16)
        for kind in range(3):
            made = jnp.dot(
                normed,
                weight_ref[kind],
                preferred_element_type=jnp.float32,
            ).T
            if kind == 0:
                q_buf[chunk] = (made * q_factor).astype(jnp.bfloat16).reshape(heads, dim, frames)
            else:
                kv_buf[chunk, :, (kind - 1) * dim : kind * dim, :] = made.astype(
                    jnp.bfloat16
                ).reshape(heads, dim, frames)
        for d in range(1, heads):
            kv_copy(chunk, d).start()
        for j in range(1, ranks):
            share_copy(chunk, 0, j).start()
        for d in range(1, seq_n):

            @pl.when(lax.rem(chunk, ranks) == lax.rem(lax.rem(me + d, seq_n), ranks))
            def _():
                q_copy(chunk, d).start()

        own_kv(chunk).start()

        @pl.when(lax.rem(chunk, ranks) == lax.rem(me, ranks))
        def _():
            own_q(chunk).start()

    for step in range(tp_n):
        chunk = lax.rem(tp - step + tp_n, tp_n)
        for d in range(1, heads):
            kv_copy(chunk, d).wait_recv()
            for j in range(1, ranks):
                share_copy(chunk, d, j).start()

    for d in range(1, tp_n):
        mix_copy(d).wait_send()
        part_copy(d).wait_send()
        cond_copy(d).wait_send()
    for chunk in range(tp_n):
        own_kv(chunk).wait()
        for d in range(1, heads):
            kv_copy(chunk, d).wait_send()
        for d in range(heads):
            for j in range(1, ranks):
                share_copy(chunk, d, j).wait()
    for k in range(tp_n // ranks):
        own_q(k * ranks).wait()
        for d in range(1, seq_n):
            q_copy(k * ranks, d).wait()


def attend_kernel(
    dims,
    natural_ref,
    place_ref,
    first_ref,
    ends_ref,
    q_ref,
    kv_ref,
    out_ref,
    key_buf,
    value_buf,
    even_buf,
    odd_buf,
):
    seq_n, tp_n, dim, block_len = dims
    frames = q_ref.shape[-1]
    per_block = block_len // frames
    block_count = place_ref.shape[0]
    tile = pl.program_id(0)
    value_rows = value_buf.shape[1]

    @pl.when(tile == 0)
    def _():
        @pl.loop(0, seq_n * tp_n)
        def _(i):
            at = pl.ds(pl.multiple_of(i * frames, frames), frames)
            key_buf[at, :] = kv_ref[i, :dim, :].astype(jnp.float32).T.astype(jnp.bfloat16)
            value_buf[i, :dim, :] = kv_ref[i, dim:, :]
            value_buf[i, dim:, :] = jnp.ones((value_rows - dim, frames), jnp.bfloat16)

    queries = q_ref[0]
    natural = natural_ref[tile]
    base = natural * block_len
    at = first_ref[tile] + lax.broadcasted_iota(jnp.int32, (1, frames), 1)
    ends = ends_ref[...]
    stop = jnp.min(jnp.where(ends > at, ends, 1 << 30), axis=0, keepdims=True)

    def score(stored, count):
        keys = key_buf[pl.ds(pl.multiple_of(stored * block_len, block_len), count), :]
        return jnp.dot(keys, queries, preferred_element_type=jnp.float32)

    def absorb(carry, *parts):
        highest, total = carry
        above = highest
        for scores, _ in parts:
            above = jnp.maximum(above, jnp.max(scores, axis=0, keepdims=True))
        total = total * jnp.exp2(highest - above)
        for scores, stored in parts:
            count = scores.shape[0]
            expo = jnp.exp2((scores - above)).astype(jnp.bfloat16)
            for c in range(pl.cdiv(count, frames)):
                size = min(frames, count - c * frames)
                total = total + jnp.dot(
                    value_buf[stored * per_block + c, :, :size],
                    expo[c * frames : c * frames + size],
                    preferred_element_type=jnp.float32,
                )
        return above, total

    def masked(scores, limit):
        row = lax.broadcasted_iota(jnp.int32, scores.shape, 0)
        return jnp.where(row < limit, scores, masked_score)

    carry = (
        jnp.full((1, frames), masked_score, jnp.float32),
        jnp.zeros((value_rows, frames), jnp.float32),
    )
    here = place_ref[natural]
    beyond = place_ref[jnp.minimum(natural + 1, block_count - 1)]
    over = jnp.where(natural + 1 < block_count, stop - base - block_len, 0)
    here_scores = score(here, block_len)
    beyond_scores = score(beyond, 128)
    even_buf[...] = score(place_ref[0], block_len)
    carry = absorb(
        carry, (masked(here_scores, stop - base), here), (masked(beyond_scores, over), beyond)
    )

    def pair(i, carry):
        odd_buf[...] = score(place_ref[2 * i + 1], block_len)
        carry = absorb(carry, (even_buf[...], place_ref[2 * i]))
        even_buf[...] = score(place_ref[2 * i + 2], block_len)
        return absorb(carry, (odd_buf[...], place_ref[2 * i + 1]))

    carry = lax.fori_loop(0, natural // 2, pair, carry)
    last = natural - lax.rem(natural, 2)
    carry = lax.fori_loop(
        last, natural, lambda j, carry: absorb(carry, (even_buf[...], place_ref[j])), carry
    )
    total = carry[1]
    out_ref[0] = (total[:dim] / total[dim : dim + 1]).astype(jnp.bfloat16)


def attend_call(dims, natural, place, first, ends, queries, keys_values):
    block_len = dims[3]
    tiles, dim, frames = queries.shape
    chunks = keys_values.shape[0]
    scores = pltpu.VMEM((block_len, frames), jnp.float32)
    return pl.pallas_call(
        functools.partial(attend_kernel, dims),
        out_shape=jax.ShapeDtypeStruct((tiles, dim, frames), jnp.bfloat16),
        grid_spec=pltpu.PrefetchScalarGridSpec(
            num_scalar_prefetch=3,
            grid=(tiles,),
            in_specs=[
                pl.BlockSpec(memory_space=pltpu.VMEM),
                pl.BlockSpec((1, dim, frames), lambda i, *_: (i, 0, 0)),
                pl.BlockSpec(memory_space=pltpu.VMEM),
            ],
            out_specs=pl.BlockSpec((1, dim, frames), lambda i, *_: (i, 0, 0)),
            scratch_shapes=[
                pltpu.VMEM((chunks * frames, dim), jnp.bfloat16),
                pltpu.VMEM((chunks, dim + 16, frames), jnp.bfloat16),
                scores,
                scores,
            ],
        ),
        compiler_params=pltpu.CompilerParams(vmem_limit_bytes=40 << 20),
        name="attend",
    )(natural, place, first, ends, queries, keys_values)


def return_kernel(dims, att_ref, out_ref, send_sem, recv_sem):
    seq_n, tp_n, heads, ranks = dims
    me = lax.axis_index("seq")
    tp = lax.axis_index("tp")
    rank = lax.rem(me, ranks)
    per = tp_n // ranks

    barrier = pltpu.get_barrier_semaphore()

    for p in range(heads):
        for t in range(tp_n):
            other = p * ranks + lax.rem(tp, ranks)

            @pl.when((other != me) | (t != tp))
            def _():
                pl.semaphore_signal(barrier, inc=1, device_id=(other, t), device_id_type=MESH)

    pl.semaphore_wait(barrier, seq_n * per - jnp.where(lax.rem(tp, ranks) == rank, 1, 0))

    mine = tp * heads + me // ranks

    def copy(i, k):
        s = lax.rem(me + i, seq_n)
        return pltpu.make_async_remote_copy(
            src_ref=att_ref.at[s, k],
            dst_ref=out_ref.at[mine],
            send_sem=send_sem.at[i, k],
            recv_sem=recv_sem.at[mine],
            device_id=(s, k * ranks + rank),
            device_id_type=MESH,
        )

    def local(k):
        return pltpu.make_async_copy(att_ref.at[me, k], out_ref.at[mine], send_sem.at[0, k])

    for i in range(seq_n):
        for k in range(per):
            if i:
                copy(i, k).start()
            else:

                @pl.when(k * ranks + rank != tp)
                def _():
                    copy(0, k).start()

                @pl.when(k * ranks + rank == tp)
                def _():
                    local(k).start()

    for i in range(seq_n):
        for k in range(per):
            if i:
                copy(i, k).wait_send()
            else:

                @pl.when(k * ranks + rank != tp)
                def _():
                    copy(0, k).wait_send()

                @pl.when(k * ranks + rank == tp)
                def _():
                    local(k).wait()

    for t in range(tp_n):
        for p in range(heads):
            source = p * ranks + lax.rem(tp, ranks)

            @pl.when((source != me) | (t != tp))
            def _():
                pltpu.make_async_remote_copy(
                    src_ref=att_ref.at[0, 0],
                    dst_ref=out_ref.at[t * heads + p],
                    send_sem=send_sem.at[0, 0],
                    recv_sem=recv_sem.at[t * heads + p],
                    device_id=(source, t),
                    device_id_type=MESH,
                ).wait_recv()


def body(
    semantic_states,
    token_projection,
    phase_offsets,
    target_spectrum,
    noise,
    timestep,
    frame_lift,
    time_weight,
    attention_weight,
    head_mixing,
    velocity_head,
    group_index,
    block_order,
):
    width = token_projection.shape[1]
    frame_count, bins = target_spectrum.shape
    upsample = phase_offsets.shape[0]
    tp_n = lax.axis_size("tp")
    seq_n = lax.axis_size("seq")
    cols = attention_weight.shape[2]
    dim = width // HEADS
    heads = cols // dim
    ranks = seq_n // heads
    per = tp_n // ranks
    tokens = semantic_states.shape[0] // tp_n
    frames_total = group_index.shape[0]
    block_count = block_order.shape[0]
    block_len = frames_total // block_count
    frames_dev = frame_count * tp_n
    blocks_dev = frames_dev // block_len
    me = lax.axis_index("seq")

    moment = timestep[0]
    mixed = ((1.0 - moment) * noise.T + moment * target_spectrum.T).astype(jnp.bfloat16)
    modulation = time_modulation(timestep, time_weight)
    mod = jnp.stack([modulation[:width], 1.0 + modulation[width:]])

    vmem = pl.BlockSpec(memory_space=pltpu.VMEM)
    hbm = pl.BlockSpec(memory_space=pl.ANY)
    dma = pltpu.SemaphoreType.DMA
    bf16 = jnp.bfloat16
    start_state, kv_all, q_all = pl.pallas_call(
        functools.partial(project_kernel, (seq_n, tp_n, heads, ranks, dim, upsample)),
        out_shape=(
            jax.ShapeDtypeStruct((frame_count, width), jnp.float32),
            jax.ShapeDtypeStruct((seq_n, tp_n, 2 * dim, frame_count), bf16),
            jax.ShapeDtypeStruct((seq_n, per, dim, frame_count), bf16),
        ),
        in_specs=[vmem] * 7,
        out_specs=(vmem, hbm, hbm),
        scratch_shapes=[
            pltpu.VMEM((tp_n, tokens, width), bf16),
            pltpu.VMEM((tp_n, tokens, width), bf16),
            pltpu.VMEM((tp_n, tokens, width), bf16),
            pltpu.VMEM((tp_n, bins, frame_count), bf16),
            pltpu.VMEM((tp_n, heads, 2 * dim, frame_count), bf16),
            pltpu.VMEM((tp_n, heads, dim, frame_count), bf16),
        ]
        + [dma((tp_n,))] * 6
        + [dma((heads, tp_n))] * 2
        + [dma((heads * ranks, tp_n))] * 2
        + [dma((seq_n, per))] * 2,
        compiler_params=pltpu.CompilerParams(
            collective_id=0, has_side_effects=True, vmem_limit_bytes=40 << 20
        ),
        name="project",
    )(
        semantic_states,
        token_projection,
        mixed,
        frame_lift,
        phase_offsets,
        mod,
        attention_weight.transpose(1, 0, 2),
    )

    head_mixing, start_state = lax.optimization_barrier((head_mixing, start_state))
    mixing = lax.all_gather(head_mixing, "tp", axis=0, tiled=True)

    group_ids = jnp.arange(frames_total // 64, dtype=jnp.int32)
    ends = jnp.sum((group_index[None, :] <= group_ids[:, None]).astype(jnp.int32), axis=1)[:, None]
    blocks = jnp.arange(block_count, dtype=jnp.int32)
    place = jnp.sum(
        jnp.where(block_order[None, :] == blocks[:, None], blocks[None, :], 0), axis=1
    ).astype(jnp.int32)
    owner = jnp.arange(per, dtype=jnp.int32) * ranks + me % ranks
    stored = (
        jnp.arange(seq_n, dtype=jnp.int32)[:, None] * blocks_dev
        + (owner * frame_count // block_len)[None, :]
    ).reshape(-1)
    natural = jnp.sum(
        jnp.where(stored[:, None] == blocks[None, :], block_order[None, :], 0), axis=1
    ).astype(jnp.int32)
    first = natural * block_len + jnp.tile(owner * frame_count % block_len, seq_n)

    tiles = seq_n * per
    attended = attend_call(
        (seq_n, tp_n, dim, block_len),
        natural,
        place,
        first,
        ends,
        q_all.reshape(tiles, dim, frame_count),
        kv_all.reshape(seq_n * tp_n, 2 * dim, frame_count),
    )

    gathered = pl.pallas_call(
        functools.partial(return_kernel, (seq_n, tp_n, heads, ranks)),
        out_shape=jax.ShapeDtypeStruct((HEADS, dim, frame_count), bf16),
        in_specs=[hbm],
        out_specs=hbm,
        scratch_shapes=[dma((seq_n, per)), dma((HEADS,))],
        compiler_params=pltpu.CompilerParams(collective_id=1, has_side_effects=True),
        name="give_back",
    )(attended.reshape(seq_n, per, dim, frame_count))

    update = lax.dot_general(
        gathered.reshape(width, frame_count),
        mixing,
        (((0,), (0,)), ((), ())),
        preferred_element_type=jnp.float32,
    )
    closing = layer_norm(start_state + update).astype(jnp.bfloat16)
    return jnp.dot(closing, velocity_head, preferred_element_type=jnp.float32)


def solution(mesh):
    in_specs = (
        P("seq", "tp"),
        P("tp", None),
        P(),
        P(("seq", "tp"), None),
        P(("seq", "tp"), None),
        P(),
        P(),
        P(),
        P(None, None, "tp"),
        P("tp", None),
        P(),
        P(),
        P(),
    )
    out_specs = P(("seq", "tp"), None)
    return jax.shard_map(body, mesh=mesh, in_specs=in_specs, out_specs=out_specs, check_vma=False)
```

```python
import functools
import math

import jax
import jax.numpy as jnp
from jax import lax
from jax.experimental import pallas as pl
from jax.experimental.pallas import tpu as pltpu
from jax.sharding import PartitionSpec as P

HEADS = 16
MESH = pl.DeviceIdType.MESH
masked_score = -1e30


def layer_norm(values):
    center = values - jnp.mean(values, axis=-1, keepdims=True)
    spread = jnp.mean(center * center, axis=-1, keepdims=True)
    return center * lax.rsqrt(spread + 1e-06)


def time_modulation(timestep, time_weight):
    half_count = time_weight.shape[0] // 2
    rates = jnp.exp(-math.log(10000.0) * jnp.arange(half_count, dtype=jnp.float32) / half_count)
    angles = 1000.0 * timestep[0] * rates
    features = jnp.concatenate([jnp.cos(angles), jnp.sin(angles)])
    return jnp.dot(jax.nn.silu(features)[None, :], time_weight, precision=lax.Precision.HIGHEST)[0]


def project_kernel(
    dims,
    states_ref,
    proj_ref,
    mixed_ref,
    lift_ref,
    phase_ref,
    mod_ref,
    weight_ref,
    start_ref,
    kv_all,
    q_all,
    part_buf,
    got_buf,
    cond_buf,
    mix_buf,
    kv_buf,
    q_buf,
    part_send,
    part_recv,
    cond_send,
    cond_recv,
    mix_send,
    mix_recv,
    kv_send,
    kv_recv,
    share_send,
    share_recv,
    q_send,
    q_recv,
):
    seq_n, tp_n, heads, ranks, dim, upsample = dims
    me = lax.axis_index("seq")
    tp = lax.axis_index("tp")
    tokens = cond_buf.shape[1]
    frames = mixed_ref.shape[1]

    barrier = pltpu.get_barrier_semaphore()
    for d in range(1, tp_n):
        pl.semaphore_signal(
            barrier, inc=1, device_id=(me, lax.rem(tp + d, tp_n)), device_id_type=MESH
        )
    for d in range(1, seq_n):
        pl.semaphore_signal(
            barrier, inc=1, device_id=(lax.rem(me + d, seq_n), tp), device_id_type=MESH
        )
    pl.semaphore_wait(barrier, tp_n - 1 + seq_n - 1)

    def tp_copy(src, dst, send, recv, d):
        return pltpu.make_async_remote_copy(
            src_ref=src,
            dst_ref=dst,
            send_sem=send.at[d],
            recv_sem=recv.at[d],
            device_id=(me, lax.rem(tp + d, tp_n)),
            device_id_type=MESH,
        )

    def mix_copy(d):
        return tp_copy(mixed_ref, mix_buf.at[d], mix_send, mix_recv, d)

    def part_copy(d):
        return tp_copy(part_buf.at[d], got_buf.at[d], part_send, part_recv, d)

    def cond_copy(d):
        return tp_copy(cond_buf.at[0], cond_buf.at[d], cond_send, cond_recv, d)

    for d in range(1, tp_n):
        mix_copy(d).start()
    mix_buf[0] = mixed_ref[...]
    own = None
    for d in list(range(1, tp_n)) + [0]:
        rows = pl.ds(pl.multiple_of(lax.rem(tp + d, tp_n) * tokens, tokens), tokens)
        piece = jnp.dot(states_ref[rows, :], proj_ref[...], preferred_element_type=jnp.float32)
        if d:
            part_buf[d] = piece.astype(jnp.bfloat16)
            part_copy(d).start()
        else:
            own = piece
    for d in range(1, tp_n):
        part_copy(d).wait_recv()
        own = own + got_buf[d].astype(jnp.float32)
    cond_buf[0] = own.astype(jnp.bfloat16)
    for d in range(1, tp_n):
        cond_copy(d).start()

    frame_at = lax.broadcasted_iota(jnp.int32, (frames, tokens), 0)
    first = lax.broadcasted_iota(jnp.int32, (frames, tokens), 1) * upsample
    spread = jnp.where((frame_at >= first) & (frame_at < first + upsample), 1.0, 0.0).astype(
        jnp.bfloat16
    )
    phase = jnp.concatenate([phase_ref[...]] * (8 // upsample), axis=0)
    q_factor = math.log2(math.e) / math.sqrt(dim)

    head = me // ranks
    rank = lax.rem(me, ranks)

    def kv_copy(chunk, d):
        goal = lax.rem(head + d, heads)
        return pltpu.make_async_remote_copy(
            src_ref=kv_buf.at[chunk, goal],
            dst_ref=kv_all.at[me, chunk],
            send_sem=kv_send.at[d, chunk],
            recv_sem=kv_recv.at[d, chunk],
            device_id=(goal * ranks + rank, tp),
            device_id_type=MESH,
        )

    def share_copy(chunk, d, j):
        source = lax.rem(head - d + heads, heads) * ranks + rank
        return pltpu.make_async_remote_copy(
            src_ref=kv_all.at[source, chunk] if d else kv_buf.at[chunk, head],
            dst_ref=kv_all.at[source, chunk],
            send_sem=share_send.at[d * ranks + j, chunk],
            recv_sem=share_recv.at[d * ranks + j, chunk],
            device_id=(head * ranks + lax.rem(rank + j, ranks), tp),
            device_id_type=MESH,
        )

    def q_copy(chunk, d):
        dest = lax.rem(me + d, seq_n)
        return pltpu.make_async_remote_copy(
            src_ref=q_buf.at[chunk, dest // ranks],
            dst_ref=q_all.at[me, chunk // ranks],
            send_sem=q_send.at[d, chunk // ranks],
            recv_sem=q_recv.at[d, chunk // ranks],
            device_id=(dest, tp),
            device_id_type=MESH,
        )

    def own_kv(chunk):
        return pltpu.make_async_copy(
            kv_buf.at[chunk, me // ranks], kv_all.at[me, chunk], kv_send.at[0, chunk]
        )

    def own_q(chunk):
        return pltpu.make_async_copy(
            q_buf.at[chunk, me // ranks],
            q_all.at[me, chunk // ranks],
            q_send.at[0, chunk // ranks],
        )

    @pl.loop(0, tp_n)
    def _(step):
        chunk = lax.rem(tp - step + tp_n, tp_n)

        @pl.when(step > 0)
        def _():
            mix_copy(step).wait_recv()
            cond_copy(step).wait_recv()

        state = lax.dot_general(
            mix_buf[step],
            lift_ref[...],
            (((0,), (0,)), ((), ())),
            preferred_element_type=jnp.float32,
        )
        state = state + jnp.dot(spread, cond_buf[step], preferred_element_type=jnp.float32)
        state = (state.reshape(frames // 8, 8, state.shape[1]) + phase[None]).reshape(state.shape)

        @pl.when(step == 0)
        def _():
            start_ref[...] = state

        normed = (layer_norm(state) * mod_ref[1:2, :] + mod_ref[0:1, :]).astype(jnp.bfloat16)
        for kind in range(3):
            made = jnp.dot(
                normed,
                weight_ref[kind],
                preferred_element_type=jnp.float32,
            ).T
            if kind == 0:
                q_buf[chunk] = (made * q_factor).astype(jnp.bfloat16).reshape(heads, dim, frames)
            else:
                kv_buf[chunk, :, (kind - 1) * dim : kind * dim, :] = made.astype(
                    jnp.bfloat16
                ).reshape(heads, dim, frames)
        for d in range(1, heads):
            kv_copy(chunk, d).start()
        for j in range(1, ranks):
            share_copy(chunk, 0, j).start()
        for d in range(1, seq_n):

            @pl.when(lax.rem(chunk, ranks) == lax.rem(lax.rem(me + d, seq_n), ranks))
            def _():
                q_copy(chunk, d).start()

        own_kv(chunk).start()

        @pl.when(lax.rem(chunk, ranks) == lax.rem(me, ranks))
        def _():
            own_q(chunk).start()

    for step in range(tp_n):
        chunk = lax.rem(tp - step + tp_n, tp_n)
        for d in range(1, heads):
            kv_copy(chunk, d).wait_recv()
            for j in range(1, ranks):
                share_copy(chunk, d, j).start()

    for d in range(1, tp_n):
        mix_copy(d).wait_send()
        part_copy(d).wait_send()
        cond_copy(d).wait_send()
    for chunk in range(tp_n):
        own_kv(chunk).wait()
        for d in range(1, heads):
            kv_copy(chunk, d).wait_send()
        for d in range(heads):
            for j in range(1, ranks):
                share_copy(chunk, d, j).wait()
    for k in range(tp_n // ranks):
        own_q(k * ranks).wait()
        for d in range(1, seq_n):
            q_copy(k * ranks, d).wait()


def attend_kernel(
    dims,
    natural_ref,
    place_ref,
    first_ref,
    ends_ref,
    q_ref,
    kv_ref,
    out_ref,
    key_buf,
    value_buf,
    even_buf,
    odd_buf,
):
    seq_n, tp_n, dim, block_len = dims
    frames = q_ref.shape[-1]
    per_block = block_len // frames
    block_count = place_ref.shape[0]
    tile = pl.program_id(0)
    value_rows = value_buf.shape[1]

    @pl.when(tile == 0)
    def _():
        @pl.loop(0, seq_n * tp_n, unroll=4)
        def _(i):
            at = pl.ds(pl.multiple_of(i * frames, frames), frames)
            key_buf[at, :] = kv_ref[i, :dim, :].astype(jnp.float32).T.astype(jnp.bfloat16)
            value_buf[i, :dim, :] = kv_ref[i, dim:, :]
            value_buf[i, dim:, :] = jnp.ones((value_rows - dim, frames), jnp.bfloat16)

    queries = q_ref[0]
    natural = natural_ref[tile]
    base = natural * block_len
    at = first_ref[tile] + lax.broadcasted_iota(jnp.int32, (1, frames), 1)
    ends = ends_ref[...]
    stop = jnp.min(jnp.where(ends > at, ends, 1 << 30), axis=0, keepdims=True)

    def score(stored, count):
        keys = key_buf[pl.ds(pl.multiple_of(stored * block_len, block_len), count), :]
        return jnp.dot(keys, queries, preferred_element_type=jnp.float32)

    def absorb(carry, *parts):
        highest, total = carry
        above = highest
        for scores, _ in parts:
            above = jnp.maximum(above, jnp.max(scores, axis=0, keepdims=True))
        total = total * jnp.exp2(highest - above)
        for scores, stored in parts:
            count = scores.shape[0]
            expo = jnp.exp2((scores - above)).astype(jnp.bfloat16)
            for c in range(pl.cdiv(count, frames)):
                size = min(frames, count - c * frames)
                total = total + jnp.dot(
                    value_buf[stored * per_block + c, :, :size],
                    expo[c * frames : c * frames + size],
                    preferred_element_type=jnp.float32,
                )
        return above, total

    def masked(scores, limit):
        row = lax.broadcasted_iota(jnp.int32, scores.shape, 0)
        return jnp.where(row < limit, scores, masked_score)

    carry = (
        jnp.full((1, frames), masked_score, jnp.float32),
        jnp.zeros((value_rows, frames), jnp.float32),
    )
    here = place_ref[natural]
    beyond = place_ref[jnp.minimum(natural + 1, block_count - 1)]
    over = jnp.where(natural + 1 < block_count, stop - base - block_len, 0)
    here_scores = score(here, block_len)
    beyond_scores = score(beyond, 128)
    even_buf[...] = score(place_ref[0], block_len)
    carry = absorb(
        carry, (masked(here_scores, stop - base), here), (masked(beyond_scores, over), beyond)
    )

    def pair(i, carry):
        odd_buf[...] = score(place_ref[2 * i + 1], block_len)
        carry = absorb(carry, (even_buf[...], place_ref[2 * i]))
        even_buf[...] = score(place_ref[2 * i + 2], block_len)
        return absorb(carry, (odd_buf[...], place_ref[2 * i + 1]))

    carry = lax.fori_loop(0, natural // 2, pair, carry)
    last = natural - lax.rem(natural, 2)
    carry = lax.fori_loop(
        last, natural, lambda j, carry: absorb(carry, (even_buf[...], place_ref[j])), carry
    )
    total = carry[1]
    out_ref[0] = (total[:dim] / total[dim : dim + 1]).astype(jnp.bfloat16)


def attend_call(dims, natural, place, first, ends, queries, keys_values):
    block_len = dims[3]
    tiles, dim, frames = queries.shape
    chunks = keys_values.shape[0]
    scores = pltpu.VMEM((block_len, frames), jnp.float32)
    return pl.pallas_call(
        functools.partial(attend_kernel, dims),
        out_shape=jax.ShapeDtypeStruct((tiles, dim, frames), jnp.bfloat16),
        grid_spec=pltpu.PrefetchScalarGridSpec(
            num_scalar_prefetch=3,
            grid=(tiles,),
            in_specs=[
                pl.BlockSpec(memory_space=pltpu.VMEM),
                pl.BlockSpec((1, dim, frames), lambda i, *_: (i, 0, 0)),
                pl.BlockSpec(memory_space=pltpu.VMEM),
            ],
            out_specs=pl.BlockSpec((1, dim, frames), lambda i, *_: (i, 0, 0)),
            scratch_shapes=[
                pltpu.VMEM((chunks * frames, dim), jnp.bfloat16),
                pltpu.VMEM((chunks, dim + 16, frames), jnp.bfloat16),
                scores,
                scores,
            ],
        ),
        compiler_params=pltpu.CompilerParams(vmem_limit_bytes=40 << 20),
        name="attend",
    )(natural, place, first, ends, queries, keys_values)


def return_kernel(dims, att_ref, out_ref, send_sem, recv_sem):
    seq_n, tp_n, heads, ranks = dims
    me = lax.axis_index("seq")
    tp = lax.axis_index("tp")
    rank = lax.rem(me, ranks)
    per = tp_n // ranks

    barrier = pltpu.get_barrier_semaphore()

    for p in range(heads):
        for t in range(tp_n):
            other = p * ranks + lax.rem(tp, ranks)

            @pl.when((other != me) | (t != tp))
            def _():
                pl.semaphore_signal(barrier, inc=1, device_id=(other, t), device_id_type=MESH)

    pl.semaphore_wait(barrier, seq_n * per - jnp.where(lax.rem(tp, ranks) == rank, 1, 0))

    mine = tp * heads + me // ranks

    def copy(i, k):
        s = lax.rem(me + i, seq_n)
        return pltpu.make_async_remote_copy(
            src_ref=att_ref.at[s, k],
            dst_ref=out_ref.at[mine],
            send_sem=send_sem.at[i, k],
            recv_sem=recv_sem.at[mine],
            device_id=(s, k * ranks + rank),
            device_id_type=MESH,
        )

    def local(k):
        return pltpu.make_async_copy(att_ref.at[me, k], out_ref.at[mine], send_sem.at[0, k])

    for i in range(seq_n):
        for k in range(per):
            if i:
                copy(i, k).start()
            else:

                @pl.when(k * ranks + rank != tp)
                def _():
                    copy(0, k).start()

                @pl.when(k * ranks + rank == tp)
                def _():
                    local(k).start()

    for i in range(seq_n):
        for k in range(per):
            if i:
                copy(i, k).wait_send()
            else:

                @pl.when(k * ranks + rank != tp)
                def _():
                    copy(0, k).wait_send()

                @pl.when(k * ranks + rank == tp)
                def _():
                    local(k).wait()

    for t in range(tp_n):
        for p in range(heads):
            source = p * ranks + lax.rem(tp, ranks)

            @pl.when((source != me) | (t != tp))
            def _():
                pltpu.make_async_remote_copy(
                    src_ref=att_ref.at[0, 0],
                    dst_ref=out_ref.at[t * heads + p],
                    send_sem=send_sem.at[0, 0],
                    recv_sem=recv_sem.at[t * heads + p],
                    device_id=(source, t),
                    device_id_type=MESH,
                ).wait_recv()


def body(
    semantic_states,
    token_projection,
    phase_offsets,
    target_spectrum,
    noise,
    timestep,
    frame_lift,
    time_weight,
    attention_weight,
    head_mixing,
    velocity_head,
    group_index,
    block_order,
):
    width = token_projection.shape[1]
    frame_count, bins = target_spectrum.shape
    upsample = phase_offsets.shape[0]
    tp_n = lax.axis_size("tp")
    seq_n = lax.axis_size("seq")
    cols = attention_weight.shape[2]
    dim = width // HEADS
    heads = cols // dim
    ranks = seq_n // heads
    per = tp_n // ranks
    tokens = semantic_states.shape[0] // tp_n
    frames_total = group_index.shape[0]
    block_count = block_order.shape[0]
    block_len = frames_total // block_count
    frames_dev = frame_count * tp_n
    blocks_dev = frames_dev // block_len
    me = lax.axis_index("seq")

    moment = timestep[0]
    mixed = ((1.0 - moment) * noise.T + moment * target_spectrum.T).astype(jnp.bfloat16)
    modulation = time_modulation(timestep, time_weight)
    mod = jnp.stack([modulation[:width], 1.0 + modulation[width:]])

    vmem = pl.BlockSpec(memory_space=pltpu.VMEM)
    hbm = pl.BlockSpec(memory_space=pl.ANY)
    dma = pltpu.SemaphoreType.DMA
    bf16 = jnp.bfloat16
    start_state, kv_all, q_all = pl.pallas_call(
        functools.partial(project_kernel, (seq_n, tp_n, heads, ranks, dim, upsample)),
        out_shape=(
            jax.ShapeDtypeStruct((frame_count, width), jnp.float32),
            jax.ShapeDtypeStruct((seq_n, tp_n, 2 * dim, frame_count), bf16),
            jax.ShapeDtypeStruct((seq_n, per, dim, frame_count), bf16),
        ),
        in_specs=[vmem] * 7,
        out_specs=(vmem, hbm, hbm),
        scratch_shapes=[
            pltpu.VMEM((tp_n, tokens, width), bf16),
            pltpu.VMEM((tp_n, tokens, width), bf16),
            pltpu.VMEM((tp_n, tokens, width), bf16),
            pltpu.VMEM((tp_n, bins, frame_count), bf16),
            pltpu.VMEM((tp_n, heads, 2 * dim, frame_count), bf16),
            pltpu.VMEM((tp_n, heads, dim, frame_count), bf16),
        ]
        + [dma((tp_n,))] * 6
        + [dma((heads, tp_n))] * 2
        + [dma((heads * ranks, tp_n))] * 2
        + [dma((seq_n, per))] * 2,
        compiler_params=pltpu.CompilerParams(
            collective_id=0, has_side_effects=True, vmem_limit_bytes=40 << 20
        ),
        name="project",
    )(
        semantic_states,
        token_projection,
        mixed,
        frame_lift,
        phase_offsets,
        mod,
        attention_weight.transpose(1, 0, 2),
    )

    head_mixing, start_state = lax.optimization_barrier((head_mixing, start_state))
    mixing = lax.all_gather(head_mixing, "tp", axis=0, tiled=True)

    group_ids = jnp.arange(frames_total // 64, dtype=jnp.int32)
    ends = jnp.sum((group_index[None, :] <= group_ids[:, None]).astype(jnp.int32), axis=1)[:, None]
    blocks = jnp.arange(block_count, dtype=jnp.int32)
    place = jnp.sum(
        jnp.where(block_order[None, :] == blocks[:, None], blocks[None, :], 0), axis=1
    ).astype(jnp.int32)
    owner = jnp.arange(per, dtype=jnp.int32) * ranks + me % ranks
    stored = (
        jnp.arange(seq_n, dtype=jnp.int32)[:, None] * blocks_dev
        + (owner * frame_count // block_len)[None, :]
    ).reshape(-1)
    natural = jnp.sum(
        jnp.where(stored[:, None] == blocks[None, :], block_order[None, :], 0), axis=1
    ).astype(jnp.int32)
    first = natural * block_len + jnp.tile(owner * frame_count % block_len, seq_n)

    tiles = seq_n * per
    attended = attend_call(
        (seq_n, tp_n, dim, block_len),
        natural,
        place,
        first,
        ends,
        q_all.reshape(tiles, dim, frame_count),
        kv_all.reshape(seq_n * tp_n, 2 * dim, frame_count),
    )

    gathered = pl.pallas_call(
        functools.partial(return_kernel, (seq_n, tp_n, heads, ranks)),
        out_shape=jax.ShapeDtypeStruct((HEADS, dim, frame_count), bf16),
        in_specs=[hbm],
        out_specs=hbm,
        scratch_shapes=[dma((seq_n, per)), dma((HEADS,))],
        compiler_params=pltpu.CompilerParams(collective_id=1, has_side_effects=True),
        name="give_back",
    )(attended.reshape(seq_n, per, dim, frame_count))

    update = lax.dot_general(
        gathered.reshape(width, frame_count),
        mixing,
        (((0,), (0,)), ((), ())),
        preferred_element_type=jnp.float32,
    )
    closing = layer_norm(start_state + update).astype(jnp.bfloat16)
    return jnp.dot(closing, velocity_head, preferred_element_type=jnp.float32)


def solution(mesh):
    in_specs = (
        P("seq", "tp"),
        P("tp", None),
        P(),
        P(("seq", "tp"), None),
        P(("seq", "tp"), None),
        P(),
        P(),
        P(),
        P(None, None, "tp"),
        P("tp", None),
        P(),
        P(),
        P(),
    )
    out_specs = P(("seq", "tp"), None)
    return jax.shard_map(body, mesh=mesh, in_specs=in_specs, out_specs=out_specs, check_vma=False)
```
